32 devices in a mesh: seq: 16 (over z, y, x), exp: 2 (over core).
Axes of the slice: x: 2, y: 2, z: 4, core: 2. Of those that a mesh axis runs over, the one named last changes fastest.
Arguments:
- queries: bfloat16 [2048, 7168], P('seq', 'exp'), may hold values from -8 to 8
- keys: bfloat16 [2048, 7168], P('seq', 'exp'), may hold values from -8 to 8
- values: bfloat16 [2048, 7168], P('seq', 'exp'), may hold values from -34 to 34
- branch_gates: float32 [2048, 2, 56], P('seq', None, 'exp'), may hold values from 0.1 to 1
- block_choice: int32 [32, 8], P('seq'), may hold values from 0 to 14, as said below
- norm_gain: float32 [7168], P('exp'), may hold values from 0.5 to 1.5
- expert_ids: int32 [2048, 8], P('seq'), may hold values from 0 to 15, all different within a row; in each aligned block of 128 rows (0 to 127, 128 to 255, ...) at most 80 rows name the same one
- route_scores: float32 [2048, 8], P('seq'), may hold values from 0.05 to 1
- w_gate_up: bfloat16 [16, 7168, 2, 1536], P('seq', 'exp'), may hold values from -0.0625 to 0.0625
- w_down: bfloat16 [16, 1536, 7168], P('seq', None, 'exp'), may hold values from -0.15625 to 0.15625
Outputs:
- mixed: bfloat16 [2048, 7168], P('seq', 'exp')
The draws below stay inside these ranges and needn't reach their ends.
Inputs may be any that keep to these rules, and one draw needn't show every extreme that they name: `block_choice`: each row holds offset 0 and 7 other distinct offsets. `expert_ids`: each row names 8 different experts; within each aligned block of 128 rows (the rows of one index of seq) no expert is named more than 80 times, and that many is reached.
All inputs are finite; a program needn't handle non-finite values.
Results may differ from the reference program's by a relative error of at most 0.029.
Values may be sent and summed in bfloat16 or wider, within the bound.
A program may use at most 128 MiB of HBM per device.

```python
import math
import jax
import jax.numpy as jnp
import numpy as np
from jax import lax

TOK_SEQ = 128
HEADS = 56
HD = 128
D = 7168
H = 1536
TOPK = 8
BLOCK = 64
TOPSEL = 8
WINDOW = 15
EXPERTS = 16
SEQ_LEN = 2048
NBLK = 32
CAP = 80
N_SEQ = 16
N_EXP = 2


def draw_queries(key, part):
    normal_part = jnp.clip(jax.random.normal(jax.random.fold_in(key, 1), (SEQ_LEN, D), jnp.float32), -3.0, 3.0)
    return normal_part.astype(jnp.bfloat16)


def draw_keys(key, part):
    normal_part = jnp.clip(jax.random.normal(jax.random.fold_in(key, 2), (SEQ_LEN, D), jnp.float32), -3.0, 3.0)
    return normal_part.astype(jnp.bfloat16)


def draw_values(key, part):
    normal_part = jnp.clip(jax.random.normal(jax.random.fold_in(key, 3), (SEQ_LEN, D), jnp.float32), -3.0, 3.0)
    jitter = jnp.exp(jax.random.uniform(jax.random.fold_in(key, 4), (HEADS,), jnp.float32, -0.22, 0.22))
    largest = 3.0
    head_scale = largest ** (jnp.arange(HEADS, dtype=jnp.float32) / (HEADS - 1)) * jitter
    shaped = normal_part.reshape(SEQ_LEN, HEADS, HD) * head_scale[None, :, None]
    return shaped.reshape(SEQ_LEN, D).astype(jnp.bfloat16)


def draw_block_choice(key, part):
    scores = jax.random.randint(jax.random.fold_in(key, 5), (NBLK, WINDOW - 1), 0, 1 << 20) * (WINDOW - 1) + jnp.arange(WINDOW - 1, dtype=jnp.int32)[None, :]
    ranking = jnp.argsort(scores, axis=1)
    others = ranking[:, :TOPSEL - 1] + 1
    return jnp.concatenate([jnp.zeros((NBLK, 1), jnp.int32), others.astype(jnp.int32)], axis=1)


def levels(key, shape, cuts, low, top_value):
    def one(position, parts):
        steps = jax.random.uniform(jax.random.fold_in(jax.random.fold_in(key, 6), position), (parts,), jnp.float32, low / len(cuts), top_value / len(cuts))
        return jnp.repeat(jnp.exp(steps), shape[position] // parts).reshape((-1,) + (1,) * (len(shape) - position - 1))

    loudness = one(*cuts[0])
    for cut in cuts[1:]:
        loudness = loudness * one(*cut)
    return loudness


def deal_out(key, own, number, rows, amount, top, most, skew):
    sequence = jax.random.permutation(key, amount)
    heavy_load, common = portions_of(amount, rows * top, most, skew, True), portions_of(amount, rows * top, most, skew, False)
    places = jnp.arange(amount)

    def named(sizes, rotation):
        used = int((sizes > 0).sum())
        fixed = max(1, used // 4)
        moved = fixed + (places - fixed + rotation * (used - fixed)) % max(1, amount - fixed)
        return jnp.zeros((amount,), jnp.int32).at[sequence[jnp.where(places < fixed, places, moved)]].set(jnp.asarray(sizes, jnp.int32))

    sizes = jnp.where(number % 4 == 0, named(heavy_load, number // 4), named(common, number - number // 4 - 1))
    mixed = jax.random.permutation(jax.random.fold_in(own, 3), amount)
    source_of, receiver = mixed[0:amount // 2 * 2:2], mixed[1:amount // 2 * 2:2]
    room = jnp.minimum(sizes[source_of] - 1, most - sizes[receiver]) // 2
    room = jnp.where((source_of == sequence[0]) | (receiver == sequence[0]) | (sizes[receiver] == 0), 0, jnp.maximum(room, 0))
    moved = jax.random.randint(jax.random.fold_in(own, 4), (amount // 2,), 0, 1 << 20) % (room + 1)
    sizes = sizes.at[source_of].add(-moved).at[receiver].add(moved)
    members = jnp.searchsorted(jnp.cumsum(sizes), jnp.arange(rows * top), side="right").astype(jnp.int32)
    listing = members.reshape(top, rows).T
    listing = listing[jax.random.permutation(jax.random.fold_in(own, 1), rows)]
    rotation = jax.random.randint(jax.random.fold_in(own, 2), (rows, 1), 0, top)
    return jnp.take_along_axis(listing, (jnp.arange(top)[None, :] + rotation) % top, axis=1)


def portions_of(number_of, total, reach, lean, full):
    portions = [(1 << 20) // math.isqrt(rank ** lean) + 1 for rank in range(1, number_of + 1)]
    largest = reach if full else min(reach, max(-(-total // number_of), total * portions[0] // sum(portions)))
    least = 1 if total - largest >= number_of - 1 else 0
    counts, rest = [largest] + [least] * (number_of - 1), total - largest - least * (number_of - 1)
    while rest > 0:
        free = [i for i in range(1, number_of) if counts[i] < largest] or [i for i in range(1, number_of) if counts[i] < reach]
        whole, remaining = sum([portions[i] for i in free]), rest
        for i in free:
            more = min(reach - counts[i], max(1, remaining * portions[i] // whole), rest)
            counts[i] = counts[i] + more
            rest = rest - more
    return np.array(counts)


def noise(own_key, extent, deviation, reach, shards=(), held_as=jnp.bfloat16):
    result = jax.random.normal(own_key, extent, jnp.float32) * deviation
    if len(shards) > 0:
        result = levels(own_key, extent, shards, -0.22, 0.18) * result
    return jnp.clip(result, min=-reach, max=reach).astype(held_as)


def setup_inputs(seed: int = 0) -> dict:
    streams_of = jax.random.split(jax.random.key(seed), 11)
    queries = draw_queries(jax.random.fold_in(streams_of[10], 71), 0)
    keys = draw_keys(jax.random.fold_in(streams_of[10], 71), 0)
    values = draw_values(jax.random.fold_in(streams_of[10], 71), 0)
    branch_gates = jnp.clip(0.1 + 0.9 * jax.random.uniform(streams_of[3], (SEQ_LEN, 2, HEADS), jnp.float32) ** levels(streams_of[3], (SEQ_LEN, 2, HEADS), ((0, 16), (2, 2)), -0.2, 0.2), 0.1, 1.0)
    block_choice = draw_block_choice(jax.random.fold_in(streams_of[10], 71), 0)
    norm_gain = jnp.clip(1.0 + 0.1 * jax.random.normal(streams_of[5], (D,), jnp.float32), 0.5, 1.5)
    expert_ids_keys = jax.random.split(jax.random.fold_in(streams_of[6], 1), SEQ_LEN // TOK_SEQ)
    expert_ids_turns = jax.random.permutation(jax.random.fold_in(streams_of[6], 3), SEQ_LEN // TOK_SEQ)
    expert_ids = jax.vmap(lambda own, number: deal_out(jax.random.fold_in(streams_of[6], 2), own, number, TOK_SEQ, EXPERTS, TOPK, CAP, 2))(expert_ids_keys, expert_ids_turns).reshape((SEQ_LEN, TOPK))
    route_scores = jnp.clip(jnp.exp(math.log(1.0) - 2.9957323 * jax.random.uniform(streams_of[7], (SEQ_LEN, TOPK), jnp.float32) ** levels(streams_of[7], (SEQ_LEN, TOPK), ((0, 16),), -0.2, 0.2)), 0.05, 1.0)
    w_gate_up = noise(streams_of[8], (EXPERTS, D, 2, H), D ** -0.5, 0.0625, ((0, 16), (1, 2)))
    w_down = noise(streams_of[9], (EXPERTS, H, D), H ** -0.5, 0.15625, ((0, 16), (2, 2)))
    return dict(queries=queries, keys=keys, values=values, branch_gates=branch_gates, block_choice=block_choice, norm_gain=norm_gain, expert_ids=expert_ids, route_scores=route_scores, w_gate_up=w_gate_up, w_down=w_down)


EPSILON = 1e-06
ROUTE_SCALE = 2.5
MASKED_SCORE = -1e+30

def rounded(x):
    return lax.optimization_barrier(x.astype(jnp.bfloat16)).astype(jnp.float32)

def coarse_branch(query_heads, pooled_keys, pooled_values, score_scale):
    seq_len = query_heads.shape[0]
    blocks = pooled_keys.shape[0]
    scores = jnp.einsum('qhd,chd->hqc', query_heads.astype(jnp.float32), pooled_keys.astype(jnp.float32)) * score_scale
    earlier = jnp.arange(blocks, dtype=jnp.int32)[None, :] < (jnp.arange(seq_len, dtype=jnp.int32) // BLOCK)[:, None]
    masked = jnp.where(earlier[None], scores, MASKED_SCORE)
    row_max = lax.optimization_barrier(jnp.max(masked, axis=2, keepdims=True))
    row_max = jnp.where(row_max > 0.5 * MASKED_SCORE, row_max, 0.0)
    weights = jnp.where(earlier[None], jnp.exp(scores - row_max), 0.0)
    weight_sum = lax.optimization_barrier(jnp.sum(weights, axis=2))
    numerator = jnp.einsum('hqc,chd->hqd', rounded(weights), pooled_values.astype(jnp.float32))
    return numerator / jnp.maximum(weight_sum, 1.0)[..., None]

def fine_branch(query_heads, key_heads, value_heads, block_choice, score_scale):
    seq_len = query_heads.shape[0]
    blocks = seq_len // BLOCK
    within = jnp.arange(BLOCK, dtype=jnp.int32)

    def one_block(block_index):
        query_rows = lax.dynamic_slice_in_dim(query_heads, block_index * BLOCK, BLOCK, 0).astype(jnp.float32)
        key_blocks = block_index - block_choice[block_index]
        reachable = key_blocks >= 0
        starts = (jnp.maximum(key_blocks, 0) * BLOCK).astype(jnp.int32)
        key_picked = jax.vmap(lambda start_row: lax.dynamic_slice_in_dim(key_heads, start_row, BLOCK, 0))(starts).astype(jnp.float32)
        value_picked = jax.vmap(lambda start_row: lax.dynamic_slice_in_dim(value_heads, start_row, BLOCK, 0))(starts).astype(jnp.float32)
        scores = jnp.einsum('qhd,skhd->hqsk', query_rows, key_picked) * score_scale
        key_pos = key_blocks[:, None] * BLOCK + within[None, :]
        query_pos = block_index * BLOCK + within
        allowed = reachable[None, :, None] & (key_pos[None, :, :] <= query_pos[:, None, None])
        masked = jnp.where(allowed[None], scores, MASKED_SCORE)
        row_max = lax.optimization_barrier(jnp.max(masked, axis=(2, 3), keepdims=True))
        weights = jnp.where(allowed[None], jnp.exp(scores - row_max), 0.0)
        weight_sum = lax.optimization_barrier(jnp.sum(weights, axis=(2, 3)))
        numerator = jnp.einsum('hqsk,skhd->hqd', rounded(weights), value_picked)
        return numerator / weight_sum[..., None]
    per_block = lax.map(one_block, jnp.arange(blocks, dtype=jnp.int32))
    return jnp.transpose(per_block, (1, 0, 2, 3)).reshape(HEADS, seq_len, HD)

def reference(queries, keys, values, branch_gates, block_choice, norm_gain, expert_ids, route_scores, w_gate_up, w_down):
    seq_len = queries.shape[0]
    blocks = seq_len // BLOCK
    score_scale = HD ** (-0.5)
    query_heads = queries.reshape(seq_len, HEADS, HD)
    key_heads = keys.reshape(seq_len, HEADS, HD)
    value_heads = values.reshape(seq_len, HEADS, HD)
    pooled_keys = lax.optimization_barrier(jnp.mean(keys.astype(jnp.float32).reshape(blocks, BLOCK, D), axis=1)).astype(jnp.bfloat16)
    pooled_values = lax.optimization_barrier(jnp.mean(values.astype(jnp.float32).reshape(blocks, BLOCK, D), axis=1)).astype(jnp.bfloat16)
    coarse_out = coarse_branch(query_heads, pooled_keys.reshape(blocks, HEADS, HD), pooled_values.reshape(blocks, HEADS, HD), score_scale)
    fine_out = fine_branch(query_heads, key_heads, value_heads, block_choice, score_scale)
    gate_coarse = jnp.transpose(branch_gates[:, 0, :])[..., None]
    gate_fine = jnp.transpose(branch_gates[:, 1, :])[..., None]
    joined = gate_coarse * coarse_out + gate_fine * fine_out
    attended = jnp.transpose(joined, (1, 0, 2)).reshape(seq_len, D).astype(jnp.bfloat16)
    wide_rows = attended.astype(jnp.float32)
    square_parts = lax.optimization_barrier(jnp.sum((wide_rows * wide_rows).reshape(seq_len, N_EXP, D // N_EXP), axis=2))
    square_sum = lax.optimization_barrier(jnp.sum(rounded(square_parts), axis=1))
    inverse_rms = lax.rsqrt(square_sum / D + EPSILON)
    normed = (wide_rows * norm_gain).astype(jnp.bfloat16)
    route_weight = ROUTE_SCALE * route_scores / lax.optimization_barrier(jnp.sum(route_scores, axis=1, keepdims=True))
    routes = expert_ids.reshape(N_SEQ, TOK_SEQ * TOPK)
    onehot = (routes[:, :, None] == jnp.arange(EXPERTS, dtype=jnp.int32)[None, None, :]).astype(jnp.int32)
    running = jnp.cumsum(onehot, axis=1) - 1
    slot_index = lax.optimization_barrier(jnp.sum(running * onehot, axis=2)).astype(jnp.int32)
    sources = jnp.broadcast_to(jnp.arange(N_SEQ, dtype=jnp.int32)[:, None], routes.shape)
    token_index = sources * TOK_SEQ + (jnp.arange(TOK_SEQ * TOPK, dtype=jnp.int32) // TOPK)[None, :]
    slot_table = jnp.full((EXPERTS, N_SEQ, CAP), -1, jnp.int32).at[routes, sources, slot_index].set(token_index)
    weight_table = jnp.zeros((EXPERTS, N_SEQ, CAP), jnp.float32).at[routes, sources, slot_index].set(route_weight.reshape(N_SEQ, TOK_SEQ * TOPK))

    def expert_step(routed, expert_index):
        row_index = slot_table[expert_index].reshape(-1)
        filled = row_index >= 0
        clamped = jnp.maximum(row_index, 0)
        picked = normed[clamped].astype(jnp.float32).reshape(-1, N_EXP, D // N_EXP)
        weight_rows = w_gate_up[expert_index].astype(jnp.float32).reshape(N_EXP, D // N_EXP, 2, H)
        partials = jnp.einsum('rnd,ndgh->rngh', picked, weight_rows)
        summed = lax.optimization_barrier(jnp.sum(rounded(partials), axis=1))
        row_scale = inverse_rms[clamped][:, None]
        activated = (jax.nn.silu(summed[:, 0] * row_scale) * (summed[:, 1] * row_scale)).astype(jnp.bfloat16)
        expert_out = rounded(jnp.dot(activated, w_down[expert_index], preferred_element_type=jnp.float32))
        row_weight = jnp.where(filled, weight_table[expert_index].reshape(-1), 0.0)
        routed = routed.at[clamped].add(row_weight[:, None] * expert_out)
        return (routed, None)
    routed, _ = lax.scan(expert_step, jnp.zeros((seq_len, D), jnp.float32), jnp.arange(EXPERTS, dtype=jnp.int32))
    return (wide_rows + routed).astype(jnp.bfloat16)
```

```python
import functools

import jax
import jax.numpy as jnp
from jax import lax
from jax.experimental import pallas as pl
from jax.experimental.pallas import tpu as pltpu
from jax.sharding import PartitionSpec as P

HD = 128
D = 7168
BLOCK = 64
WINDOW = 15


EPSILON = 1e-06
ROUTE_SCALE = 2.5
MASKED_SCORE = -1e30


def pieces(x):
    out = []
    for _ in range(3):
        part = lax.reduce_precision(x, 8, 7)
        out.append(part.astype(jnp.bfloat16))
        x = x - part
    return jnp.stack(out)


def attention_kernel(
    heads, window, q_ref, k_ref, v_ref, pk_ref, pv_ref, bias_ref, gate_ref, out_ref
):
    tile = q_ref.shape[0]
    step = pl.program_id(0)
    scale = HD ** (-0.5)
    start = pl.multiple_of(step * tile, tile)
    blocks = pk_ref.shape[0]
    bias = bias_ref[...].astype(jnp.float32)
    row = lax.broadcasted_iota(jnp.int32, (tile, blocks), 0)
    column = lax.broadcasted_iota(jnp.int32, (tile, blocks), 1)
    earlier = column < step * (tile // BLOCK) + row // BLOCK
    gates = gate_ref[...]
    contract = (((1,), (1,)), ((), ()))
    for h in range(heads):
        lanes = slice(h * HD, (h + 1) * HD)
        q = q_ref[:, lanes]
        s = lax.dot_general(
            q, k_ref[pl.ds(start, window), lanes], contract, preferred_element_type=jnp.float32
        )
        s = s * scale + bias
        m = jnp.max(s, axis=1, keepdims=True)
        w = jnp.exp(s - m)
        den = jnp.sum(w, axis=1, keepdims=True)
        fine = jnp.dot(
            w.astype(jnp.bfloat16),
            v_ref[pl.ds(start, window), lanes],
            preferred_element_type=jnp.float32,
        )
        sc = lax.dot_general(q, pk_ref[:, lanes], contract, preferred_element_type=jnp.float32)
        sc = jnp.where(earlier, sc * scale, MASKED_SCORE)
        mc = jnp.max(sc, axis=1, keepdims=True)
        mc = jnp.where(mc > 0.5 * MASKED_SCORE, mc, 0.0)
        wc = jnp.where(earlier, jnp.exp(sc - mc), 0.0)
        dc = jnp.maximum(jnp.sum(wc, axis=1, keepdims=True), 1.0)
        coarse = jnp.dot(
            wc.astype(jnp.bfloat16), pv_ref[:, lanes], preferred_element_type=jnp.float32
        )
        g0 = gates[:, h : h + 1]
        g1 = gates[:, heads + h : heads + h + 1]
        out_ref[:, lanes] = (coarse * (g0 / dc) + fine * (g1 / den)).astype(jnp.bfloat16)


def attention(queries, keys, values, branch_gates, block_choice):
    tokens, features = queries.shape
    seq = lax.axis_size("seq")
    heads_here = features // HD
    heads = -(-heads_here // seq)
    width = heads * HD
    blocks_here = tokens // BLOCK
    pad = seq * heads - heads_here

    def dealt(x):
        x = jnp.pad(x, ((0, 0), (0, pad * HD)))
        return jnp.transpose(x.reshape(tokens, seq, width), (1, 0, 2))

    gates = jnp.pad(branch_gates, ((0, 0), (0, 0), (0, pad)))
    gates = pieces(gates.reshape(tokens, 2, seq, heads))
    gates = jnp.transpose(gates, (3, 0, 2, 4, 1)).reshape(seq, -1)
    choice = jnp.broadcast_to(block_choice.reshape(1, -1), (seq, block_choice.size))
    extra = jnp.concatenate([gates, choice.astype(jnp.bfloat16)], axis=1)
    rows = -(-extra.shape[1] // (16 * width)) * 16
    extra = jnp.pad(extra, ((0, 0), (0, rows * width - extra.shape[1])))
    packed = jnp.concatenate(
        [dealt(queries), dealt(keys), dealt(values), extra.reshape(seq, rows, width)], axis=1
    )
    got = lax.all_to_all(packed, "seq", split_axis=0, concat_axis=0, tiled=True)
    q, k, v = (
        got[:, n * tokens : (n + 1) * tokens].reshape(seq * tokens, width) for n in range(3)
    )
    extra = got[:, 3 * tokens :].reshape(seq, rows * width).astype(jnp.float32)
    count = 6 * heads * tokens
    gates = jnp.sum(extra[:, :count].reshape(seq, 3, 2 * heads, tokens), axis=1)
    gates = jnp.transpose(gates, (0, 2, 1)).reshape(seq * tokens, 2 * heads)
    choice = extra[:, count : count + block_choice.size].astype(jnp.int32)
    choice = choice.reshape(seq, blocks_here, 1, block_choice.shape[1])

    before = (WINDOW - 1) * BLOCK
    window = before + tokens
    window_blocks = window // BLOCK
    gap = (
        jnp.arange(blocks_here, dtype=jnp.int32)[:, None]
        + (WINDOW - 1)
        - jnp.arange(window_blocks, dtype=jnp.int32)[None, :]
    )
    chosen = jnp.any(choice == gap[None, :, :, None], axis=3)
    inside = (
        jnp.arange(seq, dtype=jnp.int32)[:, None] * blocks_here
        + jnp.arange(window_blocks, dtype=jnp.int32)[None, :]
        >= WINDOW - 1
    )
    chosen = chosen & inside[:, None, :]
    chosen = jnp.broadcast_to(
        chosen[:, :, None, :, None], (seq, blocks_here, BLOCK, window_blocks, BLOCK)
    ).reshape(seq, tokens, window)
    causal = (
        jnp.arange(window, dtype=jnp.int32)[None, :] - before
        <= jnp.arange(tokens, dtype=jnp.int32)[:, None]
    )
    bias = jnp.where(chosen & causal[None], 0.0, MASKED_SCORE).astype(jnp.bfloat16)
    bias = bias.reshape(seq * tokens, window)

    def pooled(x):
        x = x.astype(jnp.float32).reshape(seq * blocks_here, BLOCK, width)
        return jnp.mean(x, axis=1).astype(jnp.bfloat16)

    def whole(x):
        return pl.BlockSpec(x.shape, lambda i: (0,) * x.ndim)

    pk, pv = pooled(k), pooled(v)
    kp = jnp.pad(k, ((before, 0), (0, 0)))
    vp = jnp.pad(v, ((before, 0), (0, 0)))
    out = pl.pallas_call(
        functools.partial(attention_kernel, heads, window),
        grid=(seq,),
        out_shape=jax.ShapeDtypeStruct((seq * tokens, width), jnp.bfloat16),
        in_specs=[
            pl.BlockSpec((tokens, width), lambda i: (i, 0)),
            whole(kp),
            whole(vp),
            whole(pk),
            whole(pv),
            pl.BlockSpec((tokens, window), lambda i: (i, 0)),
            pl.BlockSpec((tokens, 2 * heads), lambda i: (i, 0)),
        ],
        out_specs=pl.BlockSpec((tokens, width), lambda i: (i, 0)),
        compiler_params=pltpu.CompilerParams(vmem_limit_bytes=40 * 1024 * 1024),
    )(q, kp, vp, pk, pv, bias, gates)
    back = lax.all_to_all(
        out.reshape(seq, tokens, width), "seq", split_axis=0, concat_axis=0, tiled=True
    )
    return jnp.transpose(back, (1, 0, 2)).reshape(tokens, seq * width)[:, :features]


def local(
    queries,
    keys,
    values,
    branch_gates,
    block_choice,
    norm_gain,
    expert_ids,
    route_scores,
    w_gate_up,
    w_down,
):
    tokens_here, features = queries.shape
    seq_devices = lax.axis_size("seq")
    routes_per = expert_ids.shape[1]
    capacity = 5 * tokens_here * routes_per // (4 * seq_devices)
    named = expert_ids[:, :, None] == jnp.arange(seq_devices, dtype=jnp.int32)[None, None, :]
    member = jnp.any(named, axis=1)
    before = jnp.tri(tokens_here, k=-1, dtype=jnp.bfloat16)
    slot = jnp.dot(before, member.astype(jnp.bfloat16), preferred_element_type=jnp.float32)
    slot = jnp.where(member, slot.astype(jnp.int32), -1)
    places = jnp.arange(capacity, dtype=jnp.int32)
    at_slot = jnp.transpose(slot)[:, None, :] == places[None, :, None]
    dispatch = at_slot.astype(jnp.bfloat16).reshape(seq_devices * capacity, tokens_here)
    route_weight = ROUTE_SCALE * route_scores / jnp.sum(route_scores, axis=1, keepdims=True)
    weight = jnp.sum(jnp.where(named, route_weight[:, :, None], 0.0), axis=1)
    back_to = slot[:, :, None] == places[None, None, :]
    weight_parts = pieces(weight)[:2]
    combine = jnp.where(back_to[None], weight_parts[..., None], jnp.bfloat16(0)).reshape(
        2, tokens_here, seq_devices * capacity
    )

    hidden_state = attention(queries, keys, values, branch_gates, block_choice)
    outgoing = jnp.dot(dispatch, hidden_state, preferred_element_type=jnp.float32)
    outgoing = outgoing.astype(jnp.bfloat16).reshape(seq_devices, capacity, features)
    arrived = lax.all_to_all(outgoing, "seq", split_axis=0, concat_axis=0, tiled=True)
    sources = arrived.shape[0]
    slots = arrived.shape[1]
    wide_rows = arrived.reshape(sources * slots, features).astype(jnp.float32)
    squares = jnp.sum(wide_rows * wide_rows, axis=1)
    normed = (wide_rows * norm_gain).astype(jnp.bfloat16)
    partials = jnp.einsum("rd,dgh->rgh", normed, w_gate_up[0], preferred_element_type=jnp.float32)
    spread = jnp.broadcast_to(squares[:, None], (squares.shape[0], lax.axis_size("exp")))
    summed = lax.psum_scatter(
        partials.astype(jnp.bfloat16), "exp", scatter_dimension=2, tiled=True
    ).astype(jnp.float32)
    square_share = lax.psum_scatter(
        spread.astype(jnp.bfloat16), "exp", scatter_dimension=1, tiled=True
    ).astype(jnp.float32)
    row_scale = lax.rsqrt(square_share[:, 0] / D + EPSILON)[:, None]
    activated = (jax.nn.silu(summed[:, 0] * row_scale) * (summed[:, 1] * row_scale)).astype(
        jnp.bfloat16
    )
    down_rows = w_down[0]
    result = jnp.dot(
        lax.all_gather(activated, "exp", axis=1, tiled=True),
        down_rows,
        preferred_element_type=jnp.float32,
    )
    results_here = result.astype(jnp.bfloat16).reshape(sources, slots, features)
    returned = lax.all_to_all(results_here, "seq", split_axis=0, concat_axis=0, tiled=True)
    flattened = returned.reshape(seq_devices * capacity, features)
    routed = jnp.dot(combine[0], flattened, preferred_element_type=jnp.float32) + jnp.dot(
        combine[1], flattened, preferred_element_type=jnp.float32
    )
    return (hidden_state.astype(jnp.float32) + routed).astype(jnp.bfloat16)


def solution(mesh):
    placed = (
        P("seq", "exp"),
        P("seq", "exp"),
        P("seq", "exp"),
        P("seq", None, "exp"),
        P("seq", None),
        P("exp"),
        P("seq", None),
        P("seq", None),
        P("seq", "exp", None, None),
        P("seq", None, "exp"),
    )
    return jax.shard_map(
        local, mesh=mesh, in_specs=placed, out_specs=P("seq", "exp"), check_vma=False
    )
```

```python
import functools

import jax
import jax.numpy as jnp
from jax import lax
from jax.experimental import pallas as pl
from jax.experimental.pallas import tpu as pltpu
from jax.sharding import PartitionSpec as P

HD = 128
D = 7168
BLOCK = 64
WINDOW = 15


EPSILON = 1e-06
ROUTE_SCALE = 2.5
MASKED_SCORE = -1e30


def pieces(x):
    out = []
    for _ in range(3):
        part = lax.reduce_precision(x, 8, 7)
        out.append(part.astype(jnp.bfloat16))
        x = x - part
    return jnp.stack(out)


def attention_kernel(
    heads, window, q_ref, k_ref, v_ref, pk_ref, pv_ref, bias_ref, gate_ref, out_ref
):
    tile = q_ref.shape[0]
    step = pl.program_id(0)
    scale = HD ** (-0.5)
    start = pl.multiple_of(step * tile, tile)
    blocks = pk_ref.shape[0]
    bias = bias_ref[...].astype(jnp.float32)
    row = lax.broadcasted_iota(jnp.int32, (tile, blocks), 0)
    column = lax.broadcasted_iota(jnp.int32, (tile, blocks), 1)
    earlier = column < step * (tile // BLOCK) + row // BLOCK
    gates = gate_ref[...]
    contract = (((1,), (1,)), ((), ()))
    for h in range(heads):
        lanes = slice(h * HD, (h + 1) * HD)
        q = q_ref[:, lanes]
        s = lax.dot_general(
            q, k_ref[pl.ds(start, window), lanes], contract, preferred_element_type=jnp.float32
        )
        s = s * scale + bias
        m = jnp.max(s, axis=1, keepdims=True)
        w = jnp.exp(s - m)
        den = jnp.sum(w, axis=1, keepdims=True)
        fine = jnp.dot(
            w.astype(jnp.bfloat16),
            v_ref[pl.ds(start, window), lanes],
            preferred_element_type=jnp.float32,
        )
        sc = lax.dot_general(q, pk_ref[:, lanes], contract, preferred_element_type=jnp.float32)
        sc = jnp.where(earlier, sc * scale, MASKED_SCORE)
        mc = jnp.max(sc, axis=1, keepdims=True)
        mc = jnp.where(mc > 0.5 * MASKED_SCORE, mc, 0.0)
        wc = jnp.where(earlier, jnp.exp(sc - mc), 0.0)
        dc = jnp.maximum(jnp.sum(wc, axis=1, keepdims=True), 1.0)
        coarse = jnp.dot(
            wc.astype(jnp.bfloat16), pv_ref[:, lanes], preferred_element_type=jnp.float32
        )
        g0 = gates[:, h : h + 1]
        g1 = gates[:, heads + h : heads + h + 1]
        out_ref[:, lanes] = (coarse * (g0 / dc) + fine * (g1 / den)).astype(jnp.bfloat16)


def attention(queries, keys, values, branch_gates, block_choice):
    tokens, features = queries.shape
    seq = lax.axis_size("seq")
    heads_here = features // HD
    heads = -(-heads_here // seq)
    width = heads * HD
    blocks_here = tokens // BLOCK
    pad = seq * heads - heads_here

    def dealt(x):
        x = jnp.pad(x, ((0, 0), (0, pad * HD)))
        return jnp.transpose(x.reshape(tokens, seq, width), (1, 0, 2))

    gates = jnp.pad(branch_gates, ((0, 0), (0, 0), (0, pad)))
    gates = pieces(gates.reshape(tokens, 2, seq, heads))
    gates = jnp.transpose(gates, (3, 0, 2, 4, 1)).reshape(seq, -1)
    choice = jnp.broadcast_to(block_choice.reshape(1, -1), (seq, block_choice.size))
    extra = jnp.concatenate([gates, choice.astype(jnp.bfloat16)], axis=1)
    rows = -(-extra.shape[1] // (16 * width)) * 16
    extra = jnp.pad(extra, ((0, 0), (0, rows * width - extra.shape[1])))
    packed = jnp.concatenate(
        [dealt(queries), dealt(keys), dealt(values), extra.reshape(seq, rows, width)], axis=1
    )
    got = lax.all_to_all(packed, "seq", split_axis=0, concat_axis=0, tiled=True)
    q, k, v = (
        got[:, n * tokens : (n + 1) * tokens].reshape(seq * tokens, width) for n in range(3)
    )
    extra = got[:, 3 * tokens :].reshape(seq, rows * width).astype(jnp.float32)
    count = 6 * heads * tokens
    gates = jnp.sum(extra[:, :count].reshape(seq, 3, 2 * heads, tokens), axis=1)
    gates = jnp.transpose(gates, (0, 2, 1)).reshape(seq * tokens, 2 * heads)
    choice = extra[:, count : count + block_choice.size].astype(jnp.int32)
    choice = choice.reshape(seq, blocks_here, 1, block_choice.shape[1])

    before = (WINDOW - 1) * BLOCK
    window = before + tokens
    window_blocks = window // BLOCK
    gap = (
        jnp.arange(blocks_here, dtype=jnp.int32)[:, None]
        + (WINDOW - 1)
        - jnp.arange(window_blocks, dtype=jnp.int32)[None, :]
    )
    chosen = jnp.any(choice == gap[None, :, :, None], axis=3)
    inside = (
        jnp.arange(seq, dtype=jnp.int32)[:, None] * blocks_here
        + jnp.arange(window_blocks, dtype=jnp.int32)[None, :]
        >= WINDOW - 1
    )
    chosen = chosen & inside[:, None, :]
    expand = (
        jnp.arange(window_blocks, dtype=jnp.int32)[:, None]
        == jnp.arange(window, dtype=jnp.int32)[None, :] // BLOCK
    ).astype(jnp.bfloat16)
    chosen = jnp.dot(
        chosen.reshape(seq * blocks_here, window_blocks).astype(jnp.bfloat16),
        expand,
        preferred_element_type=jnp.float32,
    )
    chosen = jnp.broadcast_to(
        chosen.reshape(seq, blocks_here, 1, window), (seq, blocks_here, BLOCK, window)
    ).reshape(seq, tokens, window)
    causal = (
        jnp.arange(window, dtype=jnp.int32)[None, :] - before
        <= jnp.arange(tokens, dtype=jnp.int32)[:, None]
    )
    bias = jnp.where((chosen > 0.5) & causal[None], 0.0, MASKED_SCORE).astype(jnp.bfloat16)
    bias = bias.reshape(seq * tokens, window)

    def pooled(x):
        x = x.astype(jnp.float32).reshape(seq * blocks_here, BLOCK, width)
        return jnp.mean(x, axis=1).astype(jnp.bfloat16)

    def whole(x):
        return pl.BlockSpec(x.shape, lambda i: (0,) * x.ndim)

    pk, pv = pooled(k), pooled(v)
    kp = jnp.pad(k, ((before, 0), (0, 0)))
    vp = jnp.pad(v, ((before, 0), (0, 0)))
    out = pl.pallas_call(
        functools.partial(attention_kernel, heads, window),
        grid=(seq,),
        out_shape=jax.ShapeDtypeStruct((seq * tokens, width), jnp.bfloat16),
        in_specs=[
            pl.BlockSpec((tokens, width), lambda i: (i, 0)),
            whole(kp),
            whole(vp),
            whole(pk),
            whole(pv),
            pl.BlockSpec((tokens, window), lambda i: (i, 0)),
            pl.BlockSpec((tokens, 2 * heads), lambda i: (i, 0)),
        ],
        out_specs=pl.BlockSpec((tokens, width), lambda i: (i, 0)),
        compiler_params=pltpu.CompilerParams(vmem_limit_bytes=40 * 1024 * 1024),
    )(q, kp, vp, pk, pv, bias, gates)
    back = lax.all_to_all(
        out.reshape(seq, tokens, width), "seq", split_axis=0, concat_axis=0, tiled=True
    )
    return jnp.transpose(back, (1, 0, 2)).reshape(tokens, seq * width)[:, :features]


def local(
    queries,
    keys,
    values,
    branch_gates,
    block_choice,
    norm_gain,
    expert_ids,
    route_scores,
    w_gate_up,
    w_down,
):
    tokens_here, features = queries.shape
    seq_devices = lax.axis_size("seq")
    routes_per = expert_ids.shape[1]
    capacity = 5 * tokens_here * routes_per // (4 * seq_devices)
    named = expert_ids[:, :, None] == jnp.arange(seq_devices, dtype=jnp.int32)[None, None, :]
    member = jnp.any(named, axis=1)
    before = jnp.tri(tokens_here, k=-1, dtype=jnp.bfloat16)
    slot = jnp.dot(before, member.astype(jnp.bfloat16), preferred_element_type=jnp.float32)
    slot = jnp.where(member, slot.astype(jnp.int32), -1)
    route_weight = ROUTE_SCALE * route_scores / jnp.sum(route_scores, axis=1, keepdims=True)
    weight = jnp.sum(jnp.where(named, route_weight[:, :, None], 0.0), axis=1)
    weight_parts = pieces(weight)[:2]
    hidden_state = attention(queries, keys, values, branch_gates, block_choice)

    def send(first, count):
        places = first + jnp.arange(count, dtype=jnp.int32)
        at_slot = jnp.transpose(slot)[:, None, :] == places[None, :, None]
        dispatch = at_slot.astype(jnp.bfloat16).reshape(seq_devices * count, tokens_here)
        outgoing = jnp.dot(dispatch, hidden_state, preferred_element_type=jnp.float32)
        outgoing = outgoing.astype(jnp.bfloat16).reshape(seq_devices, count, features)
        return lax.all_to_all(outgoing, "seq", split_axis=0, concat_axis=0, tiled=True)

    def work(arrived):
        sources, slots = arrived.shape[:2]
        wide_rows = arrived.reshape(sources * slots, features).astype(jnp.float32)
        squares = jnp.sum(wide_rows * wide_rows, axis=1)
        normed = (wide_rows * norm_gain).astype(jnp.bfloat16)
        partials = jnp.einsum(
            "rd,dgh->rgh", normed, w_gate_up[0], preferred_element_type=jnp.float32
        )
        spread = jnp.broadcast_to(squares[:, None], (squares.shape[0], lax.axis_size("exp")))
        summed = lax.psum_scatter(
            partials.astype(jnp.bfloat16), "exp", scatter_dimension=2, tiled=True
        ).astype(jnp.float32)
        square_share = lax.psum_scatter(
            spread.astype(jnp.bfloat16), "exp", scatter_dimension=1, tiled=True
        ).astype(jnp.float32)
        row_scale = lax.rsqrt(square_share[:, 0] / D + EPSILON)[:, None]
        activated = (jax.nn.silu(summed[:, 0] * row_scale) * (summed[:, 1] * row_scale)).astype(
            jnp.bfloat16
        )
        result = jnp.dot(
            lax.all_gather(activated, "exp", axis=1, tiled=True),
            w_down[0],
            preferred_element_type=jnp.float32,
        )
        results_here = result.astype(jnp.bfloat16).reshape(sources, slots, features)
        return lax.all_to_all(results_here, "seq", split_axis=0, concat_axis=0, tiled=True)

    def combined(returned, first):
        count = returned.shape[1]
        places = first + jnp.arange(count, dtype=jnp.int32)
        back_to = slot[:, :, None] == places[None, None, :]
        combine = jnp.where(back_to[None], weight_parts[..., None], jnp.bfloat16(0))
        combine = combine.reshape(2 * tokens_here, seq_devices * count)
        both = jnp.dot(
            combine,
            returned.reshape(seq_devices * count, features),
            preferred_element_type=jnp.float32,
        )
        return both[:tokens_here] + both[tokens_here:]

    cut = -(-capacity // 32) * 16
    firsts, counts = (0, cut), (cut, capacity - cut)
    arrivals = [send(first, count) for first, count in zip(firsts, counts)]
    returns = [work(arrived) for arrived in arrivals]
    routed = combined(returns[0], firsts[0]) + combined(returns[1], firsts[1])
    return (hidden_state.astype(jnp.float32) + routed).astype(jnp.bfloat16)


def solution(mesh):
    placed = (
        P("seq", "exp"),
        P("seq", "exp"),
        P("seq", "exp"),
        P("seq", None, "exp"),
        P("seq", None),
        P("exp"),
        P("seq", None),
        P("seq", None),
        P("seq", "exp", None, None),
        P("seq", None, "exp"),
    )
    return jax.shard_map(
        local, mesh=mesh, in_specs=placed, out_specs=P("seq", "exp"), check_vma=False
    )
```
